512 devices in a mesh: row: 16 (over x_lo, y, core), col: 32 (over x_hi, z).
Axes of the slice: x: 4 (x_hi: 2, x_lo: 2; x = x_hi * 2 + x_lo), y: 4, z: 16, core: 2. Of those that a mesh axis runs over, the one named last changes fastest.
Arguments:
- eigvecs: bfloat16 [65536, 4096], P('row', 'col'), may hold values from -6 to 6
- reflectors: bfloat16 [65536, 8192], P('row', 'col'), may hold values from -0.0234375 to 0.0234375
- factors: float32 [2, 256, 256], replicated, as said below
- owners: int32 [32], replicated, may hold values from 0 to 31, each once
Outputs:
- result: bfloat16 [65536, 4096], P('row', 'col')
The draws below stay inside these ranges and needn't reach their ends.
Inputs may be any that keep to these rules, and one draw needn't show every extreme that they name: `factors`: each panel's factor is upper triangular. `owners` is a permutation of 0..31: panel p is stored in slot owners[p] for p < 2, and entries owners[2:] are not used.
All inputs are finite; a program needn't handle non-finite values.
Results may differ from the reference program's by a relative error of at most 0.0034.
Values may be sent and summed in bfloat16 or wider, within the bound.
No kernel may reach another device: no remote copies, remote signals or barrier semaphores. Data moves between devices by JAX's collectives and lax.ppermute only.
A program may use at most 64 MiB of HBM per device.

```python
import math
import jax
import jax.numpy as jnp
from jax import lax

W = 256
PANELS = 2
N = 65536
NEV = 4096
SLOTS = 8192
N_COL = 32


def draw_factors(key, part):
    key = jax.random.fold_in(key, 5)
    first, second = jax.random.split(key)
    upper = 0.3 * jax.random.normal(first, (PANELS, W, W), jnp.float32)
    diag_vals = jnp.exp(jax.random.uniform(second, (PANELS, W), jnp.float32, math.log(1.5), math.log(3.0)))
    rows = lax_iota_rows()
    above = rows[1] > rows[0]
    onto = rows[1] == rows[0]
    return jnp.where(above[None], upper, 0.0) + jnp.where(onto[None], diag_vals[:, :, None], 0.0)


def lax_iota_rows():
    line = jnp.arange(W)
    return (line[:, None] + 0 * line[None, :], line[None, :] + 0 * line[:, None])


def steps_of(stream_key, dims, cuts, smallest, high):
    def one(dim, shards_of):
        draws = jax.random.uniform(jax.random.fold_in(jax.random.fold_in(stream_key, 6), dim), (shards_of,), jnp.float32, smallest / len(cuts), high / len(cuts))
        return jnp.repeat(jnp.exp(draws), dims[dim] // shards_of).reshape((-1,) + (1,) * (len(dims) - dim - 1))

    level = one(*cuts[0])
    for cut in cuts[1:]:
        level = level * one(*cut)
    return level


def scatter_about(stream_key, dims, scale, reach, cuts=(), kind=jnp.bfloat16):
    array = scale * jax.random.normal(stream_key, dims, jnp.float32)
    if cuts:
        array = array * steps_of(stream_key, dims, cuts, -0.22, 0.18)
    return jnp.clip(array, -reach, reach).astype(kind)


def setup_inputs(seed: int = 0) -> dict:
    key_of = jax.random.split(jax.random.key(seed), 5)
    return {
        "eigvecs": scatter_about(key_of[0], (N, NEV), 1.0, 6.0, ((0, 16), (1, 32))),
        "reflectors": scatter_about(key_of[1], (N, SLOTS), N ** -0.5, 0.0234375, ((0, 16), (1, 32))),
        "factors": draw_factors(jax.random.fold_in(key_of[4], 71), 0),
        "owners": jax.random.permutation(key_of[3], N_COL).astype(jnp.int32),
    }


def reference(eigvecs, reflectors, factors, owners):
    panels = []
    for p in range(PANELS):
        start = (owners[p] * W).astype(jnp.int32)
        panels.append(lax.dynamic_slice_in_dim(reflectors, start, W, 1))
    coeffs = []
    for p in range(PANELS):
        acc = jnp.dot(panels[p].T, eigvecs, preferred_element_type=jnp.float32)
        for q in range(p):
            cross = jnp.dot(panels[p].T, panels[q], preferred_element_type=jnp.float32)
            acc = acc - jnp.dot(cross, coeffs[q].astype(jnp.float32), precision=lax.Precision.HIGHEST)
        coeffs.append(jnp.dot(factors[p], acc, precision=lax.Precision.HIGHEST).astype(jnp.bfloat16))
    total = eigvecs.astype(jnp.float32)
    for p in range(PANELS):
        total = total - jnp.dot(panels[p], coeffs[p], preferred_element_type=jnp.float32)
    return total.astype(jnp.bfloat16)
```

```python
import jax
import jax.numpy as jnp
from jax import lax
from jax.sharding import PartitionSpec as P

RING = 16
HALVES = 2
RINGS = [[half * RING + z for z in range(RING)] for half in range(HALVES)]
ACROSS = [(c, (c + RING) % (HALVES * RING)) for c in range(HALVES * RING)]


def shards(reflectors, owners):
    rows, width = reflectors.shape
    here = lax.axis_index("col") // RING
    sent = lax.all_to_all(
        reflectors.reshape(RING, rows // RING, width), "col", 0, 0, axis_index_groups=RINGS
    )
    mine = [lax.dynamic_index_in_dim(sent, owners[p] % RING, 0, False) for p in range(2)]
    theirs = lax.ppermute(jnp.stack(mine), "col", ACROSS)
    return jnp.concatenate(
        [jnp.where(owners[p] // RING == here, mine[p], theirs[p]) for p in range(2)], axis=1
    )


def contract(left, right, dims):
    return lax.dot_general(left, right, (dims, ((), ())), preferred_element_type=jnp.float32)


def sum_over_rows(part):
    count = lax.axis_size("row")
    cut = part.reshape((count, part.shape[0] // count) + part.shape[1:])
    share = jnp.sum(lax.all_to_all(cut, "row", 0, 0), axis=0)
    spread = jnp.broadcast_to(share[None], (count,) + share.shape)
    return lax.all_to_all(spread, "row", 0, 0).reshape(part.shape)


def exact(left, right):
    return lax.dot_general(
        left, right, (((1,), (1,)), ((), ())), precision=lax.Precision.HIGHEST,
        preferred_element_type=jnp.float32,
    )


def per_device(eigvecs, reflectors, factors, owners):
    width = reflectors.shape[1]
    columns = eigvecs.shape[1]
    panels = lax.all_gather(
        shards(reflectors, owners), "col", tiled=True, axis_index_groups=RINGS
    )
    proj = contract(eigvecs, panels, ((0,), (0,)))
    cross = contract(panels[:, width:], panels[:, :width], ((0,), (0,)))
    packed = jnp.concatenate([proj[:, :width], proj[:, width:], cross], axis=0)
    summed = sum_over_rows(packed)
    first, second = summed[:columns], summed[columns : 2 * columns]
    cross = summed[2 * columns :]
    lead = exact(first, factors[0]).astype(jnp.bfloat16)
    rest = second - exact(lead.astype(jnp.float32), cross)
    tail = exact(rest, factors[1]).astype(jnp.bfloat16)
    coeffs = jnp.concatenate([lead, tail], axis=1)
    update = contract(panels, coeffs, ((1,), (1,)))
    return (eigvecs.astype(jnp.float32) - update).astype(jnp.bfloat16)


def solution(mesh):
    placed = (P("row", "col"), P("row", "col"), P(), P())
    return jax.shard_map(
        per_device, mesh=mesh, in_specs=placed, out_specs=P("row", "col"), check_vma=False
    )
```

```python
import jax
import jax.numpy as jnp
from jax import lax
from jax.sharding import PartitionSpec as P

RING = 16
HALVES = 2
RINGS = [[half * RING + z for z in range(RING)] for half in range(HALVES)]
ACROSS = [(c, (c + RING) % (HALVES * RING)) for c in range(HALVES * RING)]


def step(block, by, cycle=1, place=0):
    pairs = [
        (half * RING + z, half * RING + (z + by) % RING)
        for half in range(HALVES)
        for z in range(place % cycle, RING, cycle)
    ]
    return lax.ppermute(block, "col", pairs)


def pick(index, choices):
    out = choices[0]
    for k in range(1, len(choices)):
        out = jnp.where(index == k, choices[k], out)
    return out


def scatter_from(places):
    def run(quarters, offsets, z):
        sent = {}
        held = []
        for p in range(2):
            for k, by, cycle in ((1, 4, 4), (3, -4, 4), (2, 8, 8)):
                key = (k, places[p] % cycle)
                if key not in sent:
                    sent[key] = step(quarters[k], by, cycle, places[p])
        for p in range(2):
            got = [quarters[0]] + [
                sent[k, places[p] % cycle] for k, cycle in ((1, 4), (2, 8), (3, 4))
            ]
            held.append(pick(offsets[p] // 4, got))
        classes = [place % 4 for place in places]
        if classes[0] != classes[1]:
            slots = jnp.where(z % 4 == classes[0], held[0], held[1])[None]
        else:
            slots = jnp.stack(held)
        after = step(slots[:, 2], 1)
        before = step(slots[:, 0], -1)
        second = step(slots[:, 3], 2)
        last = slots.shape[0] - 1
        out = []
        for p in range(2):
            s = min(p, last)
            out.append(
                pick((z - classes[p]) % 4, [slots[s, 1], after[s], second[s], before[s]])
            )
        return jnp.stack(out)

    return run


def shards(reflectors, owners):
    rows, width = reflectors.shape
    here = lax.axis_index("col") // RING
    z = lax.axis_index("col") % RING
    blocks = reflectors.reshape(RING, rows // RING, width)
    quarters = [
        jnp.stack(
            [
                lax.dynamic_index_in_dim(blocks, (z + 4 * k + j) % RING, 0, False)
                for j in (RING - 1, 0, 1, 2)
            ]
        )
        for k in range(4)
    ]
    offsets = [(z - owners[p] + HALVES * RING) % RING for p in range(2)]
    branches = [scatter_from((a, b)) for a in range(8) for b in range(8)]
    which = (owners[0] % 8) * 8 + owners[1] % 8
    mine = lax.switch(which, branches, quarters, offsets, z)
    theirs = lax.ppermute(mine, "col", ACROSS)
    return jnp.concatenate(
        [jnp.where(owners[p] // RING == here, mine[p], theirs[p]) for p in range(2)], axis=1
    )


def contract(left, right, dims):
    return lax.dot_general(left, right, (dims, ((), ())), preferred_element_type=jnp.float32)


def sum_over_rows(part):
    count = lax.axis_size("row")
    cut = part.reshape((count, part.shape[0] // count) + part.shape[1:])
    share = jnp.sum(lax.all_to_all(cut, "row", 0, 0), axis=0)
    spread = jnp.broadcast_to(share[None], (count,) + share.shape)
    return lax.all_to_all(spread, "row", 0, 0).reshape(part.shape)


def exact(left, right):
    return lax.dot_general(
        left, right, (((1,), (1,)), ((), ())), precision=lax.Precision.HIGHEST,
        preferred_element_type=jnp.float32,
    )


def per_device(eigvecs, reflectors, factors, owners):
    width = reflectors.shape[1]
    columns = eigvecs.shape[1]
    panels = lax.all_gather(
        shards(reflectors, owners), "col", tiled=True, axis_index_groups=RINGS
    )
    proj = contract(eigvecs, panels, ((0,), (0,)))
    cross = contract(panels[:, width:], panels[:, :width], ((0,), (0,)))
    packed = jnp.concatenate([proj[:, :width], proj[:, width:], cross], axis=0)
    summed = sum_over_rows(packed)
    first, second = summed[:columns], summed[columns : 2 * columns]
    cross = summed[2 * columns :]
    lead = exact(first, factors[0]).astype(jnp.bfloat16)
    rest = second - exact(lead.astype(jnp.float32), cross)
    tail = exact(rest, factors[1]).astype(jnp.bfloat16)
    coeffs = jnp.concatenate([lead, tail], axis=1)
    update = contract(panels, coeffs, ((1,), (1,)))
    return (eigvecs.astype(jnp.float32) - update).astype(jnp.bfloat16)


def solution(mesh):
    placed = (P("row", "col"), P("row", "col"), P(), P())
    return jax.shard_map(
        per_device, mesh=mesh, in_specs=placed, out_specs=P("row", "col"), check_vma=False
    )
```

```python
import jax
import jax.numpy as jnp
from jax import lax
from jax.sharding import PartitionSpec as P

RING = 16
HALVES = 2
RINGS = [[half * RING + z for z in range(RING)] for half in range(HALVES)]
PAIRS = [[z, z + RING] for z in range(RING)]
SCALE = 2.0**21


def gather_panels(reflectors, owners):
    z = lax.axis_index("col") % RING
    block = (reflectors.astype(jnp.float32) * SCALE).astype(jnp.float16)
    both = lax.all_gather(block, "col", axis_index_groups=PAIRS)
    sent = []
    for p in range(2):
        tile = lax.dynamic_index_in_dim(both, owners[p] // RING, 0, False)
        sent.append(jnp.where(owners[p] % RING == z, tile, jnp.zeros_like(tile)))
    whole = lax.psum(jnp.concatenate(sent, axis=1), "col", axis_index_groups=RINGS)
    return whole.astype(jnp.bfloat16)


def contract(left, right, dims):
    return lax.dot_general(left, right, (dims, ((), ())), preferred_element_type=jnp.float32)


def sum_over_rows(part):
    count = lax.axis_size("row")
    cut = part.reshape((count, part.shape[0] // count) + part.shape[1:])
    share = jnp.sum(lax.all_to_all(cut, "row", 0, 0), axis=0)
    spread = jnp.broadcast_to(share[None], (count,) + share.shape)
    return lax.all_to_all(spread, "row", 0, 0).reshape(part.shape)


def exact(left, right):
    return lax.dot_general(
        left, right, (((1,), (1,)), ((), ())), precision=lax.Precision.HIGHEST,
        preferred_element_type=jnp.float32,
    )


def per_device(eigvecs, reflectors, factors, owners):
    width = reflectors.shape[1]
    columns = eigvecs.shape[1]
    panels = gather_panels(reflectors, owners)
    proj = contract(eigvecs, panels, ((0,), (0,)))
    cross = contract(panels[:, width:], panels[:, :width], ((0,), (0,)))
    packed = jnp.concatenate([proj[:, :width], proj[:, width:], cross], axis=0)
    summed = sum_over_rows(packed)
    first = summed[:columns] * (1 / SCALE)
    second = summed[columns : 2 * columns] * (1 / SCALE)
    cross = summed[2 * columns :] * (1 / SCALE**2)
    lead = exact(first, factors[0]).astype(jnp.bfloat16)
    rest = second - exact(lead.astype(jnp.float32), cross)
    tail = exact(rest, factors[1]).astype(jnp.bfloat16)
    coeffs = jnp.concatenate([lead, tail], axis=1)
    update = contract(panels, coeffs, ((1,), (1,)))
    return (eigvecs.astype(jnp.float32) - update * (1 / SCALE)).astype(jnp.bfloat16)


def solution(mesh):
    placed = (P("row", "col"), P("row", "col"), P(), P())
    return jax.shard_map(
        per_device, mesh=mesh, in_specs=placed, out_specs=P("row", "col"), check_vma=False
    )
```

```python
import jax
import jax.numpy as jnp
from jax import lax
from jax.sharding import Mesh, PartitionSpec as P

RING = 16
HALVES = 2
SUMMED = ("row", "half")
SCALE = 2.0**21


def gather_panels(reflectors, owners):
    z = lax.axis_index("z")
    rows, width = reflectors.shape
    block = (reflectors.astype(jnp.float32) * SCALE).astype(jnp.float16)
    both = lax.all_to_all(block.reshape(HALVES, rows // HALVES, width), "half", 0, 0)
    sent = []
    for p in range(2):
        tile = lax.dynamic_index_in_dim(both, owners[p] // RING, 0, False)
        sent.append(jnp.where(owners[p] % RING == z, tile, jnp.zeros_like(tile)))
    whole = lax.psum(jnp.concatenate(sent, axis=1), "z")
    return whole.astype(jnp.bfloat16)


def contract(left, right, dims):
    return lax.dot_general(left, right, (dims, ((), ())), preferred_element_type=jnp.float32)


def sum_over(part, axes):
    count = lax.axis_size(axes)
    cut = part.reshape((count, part.shape[0] // count) + part.shape[1:])
    share = jnp.sum(lax.all_to_all(cut, axes, 0, 0), axis=0)
    spread = jnp.broadcast_to(share[None], (count,) + share.shape)
    return lax.all_to_all(spread, axes, 0, 0).reshape(part.shape)


def exact(left, right):
    return lax.dot_general(
        left, right, (((1,), (1,)), ((), ())), precision=lax.Precision.HIGHEST,
        preferred_element_type=jnp.float32,
    )


def swap(block):
    return lax.ppermute(block, "half", [(0, 1), (1, 0)])


def per_device(eigvecs, reflectors, factors, owners):
    rows, columns = eigvecs.shape
    width = reflectors.shape[1]
    half = lax.axis_index("half")
    tiles = eigvecs.reshape(HALVES, rows // HALVES, columns)
    mine = lax.dynamic_index_in_dim(tiles, half, 0, False)
    theirs = swap(lax.dynamic_index_in_dim(tiles, 1 - half, 0, False))
    panels = gather_panels(reflectors, owners)

    def projected(tile):
        return contract(tile, panels, ((0,), (0,)))

    here, there = projected(mine), projected(theirs)
    cross = contract(panels[:, width:], panels[:, :width], ((0,), (0,)))
    lower = jnp.where(half == 0, here, there)
    upper = jnp.where(half == 0, there, here)
    packed = jnp.concatenate(
        [lower[:, :width], upper[:, :width], lower[:, width:], upper[:, width:], cross], axis=0
    )
    summed = sum_over(packed, SUMMED)
    count = HALVES * columns
    first = summed[:count] * (1 / SCALE)
    second = summed[count : 2 * count] * (1 / SCALE)
    cross = summed[2 * count :] * (1 / SCALE**2)
    lead = exact(first, factors[0]).astype(jnp.bfloat16)
    rest = second - exact(lead.astype(jnp.float32), cross)
    tail = exact(rest, factors[1]).astype(jnp.bfloat16)
    coeffs = jnp.concatenate([lead, tail], axis=1).reshape(HALVES, columns, 2 * width)

    def updated(tile, which):
        part = lax.dynamic_index_in_dim(coeffs, which, 0, False)
        update = contract(panels, part, ((1,), (1,)))
        return (tile.astype(jnp.float32) - update * (1 / SCALE)).astype(jnp.bfloat16)

    got = swap(updated(theirs, 1 - half))
    kept = updated(mine, half)
    first_rows = jnp.where(half == 0, kept, got)
    last_rows = jnp.where(half == 0, got, kept)
    return jnp.concatenate([first_rows, last_rows], axis=0)


def solution(mesh):
    fine = Mesh(mesh.devices.reshape(-1, HALVES, RING), ("row", "half", "z"))
    tiled = P("row", ("half", "z"))
    return jax.shard_map(
        per_device, mesh=fine, in_specs=(tiled, tiled, P(), P()), out_specs=tiled, check_vma=False
    )
```

```python
import jax
import jax.numpy as jnp
from jax import lax
from jax.sharding import Mesh, PartitionSpec as P

RING = 16
HALVES = 2
SUMMED = ("row", "half")
SCALE = 2.0**21


def swap(block):
    return lax.ppermute(block, "half", [(0, 1), (1, 0)])


def parts_of(tile, half):
    rows = tile.shape[0] // HALVES
    halves = tile.reshape(HALVES, rows, tile.shape[1])
    return (
        lax.dynamic_index_in_dim(halves, half, 0, False),
        lax.dynamic_index_in_dim(halves, 1 - half, 0, False),
    )


def spread_panels(own, other, owners, half):
    slot = owners[:2].reshape(2, 1, 1)
    level = jnp.where(slot % RING == lax.axis_index("z"), SCALE, 0.0)
    from_own = jnp.where(slot // RING == half, level, 0.0)
    from_other = jnp.where(slot // RING == half, 0.0, level)
    sent = own.astype(jnp.float32) * from_own + other.astype(jnp.float32) * from_other
    return lax.psum(sent.astype(jnp.float16), "z").astype(jnp.bfloat16)


def contract(left, right, dims):
    return lax.dot_general(left, right, (dims, ((), ())), preferred_element_type=jnp.float32)


def sum_over(part, axes):
    count = lax.axis_size(axes)
    cut = part.reshape((count, part.shape[0] // count) + part.shape[1:])
    share = jnp.sum(lax.all_to_all(cut, axes, 0, 0), axis=0)
    spread = jnp.broadcast_to(share[None], (count,) + share.shape)
    return lax.all_to_all(spread, axes, 0, 0).reshape(part.shape)


def exact(left, right):
    return lax.dot_general(
        left, right, (((1,), (1,)), ((), ())), precision=lax.Precision.HIGHEST,
        preferred_element_type=jnp.float32,
    )


def per_device(eigvecs, reflectors, factors, owners):
    columns = eigvecs.shape[1]
    half = lax.axis_index("half")
    own, away = parts_of(reflectors, half)
    other = swap(away)
    mine, guest = parts_of(eigvecs, half)
    other, guest = lax.optimization_barrier((other, guest))
    theirs = swap(guest)
    panels = spread_panels(own, other, owners, half)

    blocks = []
    for p in range(2):
        here = contract(mine, panels[p], ((0,), (0,)))
        there = contract(theirs, panels[p], ((0,), (0,)))
        blocks += [jnp.where(half == 0, here, there), jnp.where(half == 0, there, here)]
    cross = contract(panels[1], panels[0], ((0,), (0,)))
    summed = sum_over(jnp.concatenate(blocks + [cross], axis=0), SUMMED)
    count = HALVES * columns
    first = summed[:count] * (1 / SCALE)
    second = summed[count : 2 * count] * (1 / SCALE)
    cross = summed[2 * count :] * (1 / SCALE**2)
    lead = exact(first, factors[0]).astype(jnp.bfloat16)
    rest = second - exact(lead.astype(jnp.float32), cross)
    tail = exact(rest, factors[1]).astype(jnp.bfloat16)
    coeffs = [part.reshape(HALVES, columns, part.shape[1]) for part in (lead, tail)]

    def updated(tile, which):
        total = tile.astype(jnp.float32)
        for p in range(2):
            part = lax.dynamic_index_in_dim(coeffs[p], which, 0, False)
            total = total - contract(panels[p], part, ((1,), (1,))) * (1 / SCALE)
        return total.astype(jnp.bfloat16)

    got = swap(updated(theirs, 1 - half))
    kept = updated(mine, half)
    first_rows = jnp.where(half == 0, kept, got)
    last_rows = jnp.where(half == 0, got, kept)
    return jnp.concatenate([first_rows, last_rows], axis=0)


def solution(mesh):
    fine = Mesh(mesh.devices.reshape(-1, HALVES, RING), ("row", "half", "z"))
    tiled = P("row", ("half", "z"))
    return jax.shard_map(
        per_device, mesh=fine, in_specs=(tiled, tiled, P(), P()), out_specs=tiled, check_vma=False
    )
```

```python
import jax
import jax.numpy as jnp
from jax import lax
from jax.sharding import Mesh, PartitionSpec as P

RING = 16
HALVES = 2
SCALE = 2.0**21


def swap(block, axis="half"):
    return lax.ppermute(block, axis, [(0, 1), (1, 0)])


def parts_of(tile, half):
    rows = tile.shape[0] // HALVES
    halves = tile.reshape(HALVES, rows, tile.shape[1])
    return (
        lax.dynamic_index_in_dim(halves, half, 0, False),
        lax.dynamic_index_in_dim(halves, 1 - half, 0, False),
    )


def spread_panels(own, other, owners, half):
    slot = owners[:2].reshape(2, 1, 1)
    block = jnp.where(slot // RING == half, own[None], other[None])
    sent = jnp.where(slot % RING == lax.axis_index("z"), block, jnp.zeros_like(block))
    scaled = (sent.astype(jnp.float32) * SCALE).astype(jnp.float16)
    return lax.psum(scaled, "z")


def contract(left, right, dims):
    return lax.dot_general(left, right, (dims, ((), ())), preferred_element_type=jnp.float32)


def sum_over(part, axes):
    count = lax.axis_size(axes)
    cut = part.reshape((count, part.shape[0] // count) + part.shape[1:])
    share = jnp.sum(lax.all_to_all(cut, axes, 0, 0), axis=0)
    spread = jnp.broadcast_to(share[None], (count,) + share.shape)
    return lax.all_to_all(spread, axes, 0, 0).reshape(part.shape)


def sum_over_rows(part):
    core = lax.axis_index("core")
    keep, give = parts_of(part, core)
    kept = sum_over(keep + swap(give, "core"), ("chip", "half"))
    rest = swap(kept, "core")
    return jnp.concatenate(
        [jnp.where(core == 0, kept, rest), jnp.where(core == 0, rest, kept)], axis=0
    )


def exact(left, right):
    return lax.dot_general(
        left, right, (((1,), (1,)), ((), ())), precision=lax.Precision.HIGHEST,
        preferred_element_type=jnp.float32,
    )


def per_device(eigvecs, reflectors, factors, owners):
    columns = eigvecs.shape[1]
    half = lax.axis_index("half")
    own, away = parts_of(reflectors, half)
    other = swap(away)
    mine, guest = parts_of(eigvecs, half)
    theirs = swap(guest)
    whole = spread_panels(own, other, owners, half)
    panels = [whole[p].astype(jnp.bfloat16) for p in range(2)]

    blocks = []
    for p in range(2):
        here = contract(mine, panels[p], ((0,), (0,)))
        there = contract(theirs, panels[p], ((0,), (0,)))
        blocks += [jnp.where(half == 0, here, there), jnp.where(half == 0, there, here)]
    cross = contract(panels[1], panels[0], ((0,), (0,)))
    summed = sum_over_rows(jnp.concatenate(blocks + [cross], axis=0))
    count = HALVES * columns
    first = summed[:count] * (1 / SCALE)
    second = summed[count : 2 * count] * (1 / SCALE)
    cross = summed[2 * count :] * (1 / SCALE**2)
    lead = exact(first, factors[0]).astype(jnp.bfloat16)
    rest = second - exact(lead.astype(jnp.float32), cross)
    tail = exact(rest, factors[1]).astype(jnp.bfloat16)
    coeffs = [part.reshape(HALVES, columns, part.shape[1]) for part in (lead, tail)]

    def updated(tile, which):
        total = tile.astype(jnp.float32)
        for p in range(2):
            part = lax.dynamic_index_in_dim(coeffs[p], which, 0, False)
            total = total - contract(panels[p], part, ((1,), (1,))) * (1 / SCALE)
        return total.astype(jnp.bfloat16)

    got = swap(updated(theirs, 1 - half))
    kept = updated(mine, half)
    first_rows = jnp.where(half == 0, kept, got)
    last_rows = jnp.where(half == 0, got, kept)
    return jnp.concatenate([first_rows, last_rows], axis=0)


def solution(mesh):
    fine = Mesh(mesh.devices.reshape(-1, 2, HALVES, RING), ("chip", "core", "half", "z"))
    tiled = P(("chip", "core"), ("half", "z"))
    return jax.shard_map(
        per_device, mesh=fine, in_specs=(tiled, tiled, P(), P()), out_specs=tiled, check_vma=False
    )
```

```python
import jax
import jax.numpy as jnp
from jax import lax
from jax.sharding import Mesh, PartitionSpec as P

RING = 16
HALVES = 2
SCALE = 2.0**21


def swap(block):
    return lax.ppermute(block, "half", [(0, 1), (1, 0)])


def parts_of(tile, half):
    rows = tile.shape[0] // HALVES
    halves = tile.reshape(HALVES, rows, tile.shape[1])
    return (
        lax.dynamic_index_in_dim(halves, half, 0, False),
        lax.dynamic_index_in_dim(halves, 1 - half, 0, False),
    )


def spread_panels(own, other, owners, half):
    slot = owners[:2].reshape(2, 1, 1)
    block = jnp.where(slot // RING == half, own[None], other[None])
    sent = jnp.where(slot % RING == lax.axis_index("z"), block, jnp.zeros_like(block))
    scaled = (sent.astype(jnp.float32) * SCALE).astype(jnp.float16)
    return lax.psum(scaled, "z")


def contract(left, right, dims):
    return lax.dot_general(left, right, (dims, ((), ())), preferred_element_type=jnp.float32)


def sum_over(part, axes):
    count = lax.axis_size(axes)
    cut = part.reshape((count, part.shape[0] // count) + part.shape[1:])
    share = jnp.sum(lax.all_to_all(cut, axes, 0, 0), axis=0)
    spread = jnp.broadcast_to(share[None], (count,) + share.shape)
    return lax.all_to_all(spread, axes, 0, 0).reshape(part.shape)


def exact(left, right):
    return lax.dot_general(
        left, right, (((1,), (1,)), ((), ())), precision=lax.Precision.HIGHEST,
        preferred_element_type=jnp.float32,
    )


def per_device(eigvecs, reflectors, factors, owners):
    columns = eigvecs.shape[1]
    half = lax.axis_index("half")
    own, away = parts_of(reflectors, half)
    other = swap(away)
    mine, guest = parts_of(eigvecs, half)
    theirs = swap(guest)
    whole = spread_panels(own, other, owners, half)
    panels = [whole[p].astype(jnp.bfloat16) for p in range(2)]

    blocks = []
    for p in range(2):
        here = contract(mine, panels[p], ((0,), (0,)))
        there = contract(theirs, panels[p], ((0,), (0,)))
        blocks += [jnp.where(half == 0, here, there), jnp.where(half == 0, there, here)]
    cross = contract(panels[1], panels[0], ((0,), (0,)))
    packed = jnp.concatenate(blocks + [cross], axis=0)
    far = swap(whole)
    summed = sum_over(packed, ("row", "half"))
    count = HALVES * columns
    first = summed[:count] * (1 / SCALE)
    second = summed[count : 2 * count] * (1 / SCALE)
    cross = summed[2 * count :] * (1 / SCALE**2)
    lead = exact(first, factors[0]).astype(jnp.bfloat16)
    rest = second - exact(lead.astype(jnp.float32), cross)
    tail = exact(rest, factors[1]).astype(jnp.bfloat16)
    coeffs = [
        lax.dynamic_index_in_dim(part.reshape(HALVES, columns, part.shape[1]), half, 0, False)
        for part in (lead, tail)
    ]

    def updated(tile, side):
        total = tile.astype(jnp.float32)
        for p in range(2):
            update = contract(side[p].astype(jnp.bfloat16), coeffs[p], ((1,), (1,)))
            total = total - update * (1 / SCALE)
        return total.astype(jnp.bfloat16)

    near = updated(mine, whole)
    rest = updated(guest, far)
    result = jnp.stack([jnp.where(half == 0, near, rest), jnp.where(half == 0, rest, near)])
    return result.reshape(eigvecs.shape)


def solution(mesh):
    fine = Mesh(mesh.devices.reshape(-1, HALVES, RING), ("row", "half", "z"))
    tiled = P("row", ("half", "z"))
    return jax.shard_map(
        per_device, mesh=fine, in_specs=(tiled, tiled, P(), P()), out_specs=tiled, check_vma=False
    )
```

```python
import jax
import jax.numpy as jnp
from jax import lax
from jax.sharding import Mesh, PartitionSpec as P

RING = 16
HALVES = 2
SCALE = 2.0**21


def swap(block):
    return lax.ppermute(block, "half", [(0, 1), (1, 0)])


def part_of(tile, half):
    rows = tile.shape[0] // HALVES
    return lax.dynamic_index_in_dim(tile.reshape(HALVES, rows, tile.shape[1]), half, 0, False)


def by_half(first, second, half):
    place = jnp.arange(HALVES).reshape((HALVES,) + (1,) * first.ndim)
    return jnp.where(place == half, first[None], second[None])


def spread_panels(own, other, owners, half):
    slot = owners[:2].reshape(2, 1, 1)
    block = jnp.where(slot // RING == half, own[None], other[None])
    sent = jnp.where(slot % RING == lax.axis_index("z"), block, jnp.zeros_like(block))
    scaled = (sent.astype(jnp.float32) * SCALE).astype(jnp.float16)
    return lax.psum(scaled, "z")


def contract(left, right, dims):
    return lax.dot_general(left, right, (dims, ((), ())), preferred_element_type=jnp.float32)


def sum_over(part, axes):
    count = lax.axis_size(axes)
    cut = part.reshape((count, part.shape[0] // count) + part.shape[1:])
    share = jnp.sum(lax.all_to_all(cut, axes, 0, 0), axis=0)
    spread = jnp.broadcast_to(share[None], (count,) + share.shape)
    return lax.all_to_all(spread, axes, 0, 0).reshape(part.shape)


def exact(left, right):
    return lax.dot_general(
        left, right, (((1,), (1,)), ((), ())), precision=lax.Precision.HIGHEST,
        preferred_element_type=jnp.float32,
    )


def per_device(eigvecs, reflectors, factors, owners):
    columns, width = eigvecs.shape[1], reflectors.shape[1]
    half = lax.axis_index("half")
    other = swap(part_of(reflectors, 1 - half))
    theirs = swap(part_of(eigvecs, 1 - half))
    reflectors, other = lax.optimization_barrier((reflectors, other))
    own = part_of(reflectors, half)
    mine = part_of(eigvecs, half)
    whole = spread_panels(own, other, owners, half)
    panels = [whole[p].astype(jnp.bfloat16) for p in range(2)]

    blocks = []
    for p in range(2):
        here = contract(mine, panels[p], ((0,), (0,)))
        there = contract(theirs, panels[p], ((0,), (0,)))
        blocks.append(by_half(here, there, half).reshape(HALVES * columns, width))
    cross = contract(panels[1], panels[0], ((0,), (0,)))
    summed = sum_over(jnp.concatenate(blocks + [cross], axis=0), ("row", "half"))
    count = HALVES * columns
    first = summed[:count] * (1 / SCALE)
    second = summed[count : 2 * count] * (1 / SCALE)
    cross = summed[2 * count :] * (1 / SCALE**2)
    lead = exact(first, factors[0]).astype(jnp.bfloat16)
    rest = second - exact(lead.astype(jnp.float32), cross)
    tail = exact(rest, factors[1]).astype(jnp.bfloat16)
    coeffs = [part.reshape(HALVES, columns, part.shape[1]) for part in (lead, tail)]

    def updated(tile, which):
        total = tile.astype(jnp.float32)
        for p in range(2):
            part = lax.dynamic_index_in_dim(coeffs[p], which, 0, False)
            total = total - contract(panels[p], part, ((1,), (1,))) * (1 / SCALE)
        return total.astype(jnp.bfloat16)

    got = swap(updated(theirs, 1 - half))
    kept = updated(mine, half)
    return by_half(kept, got, half).reshape(eigvecs.shape)


def solution(mesh):
    fine = Mesh(mesh.devices.reshape(-1, HALVES, RING), ("row", "half", "z"))
    tiled = P("row", ("half", "z"))
    return jax.shard_map(
        per_device, mesh=fine, in_specs=(tiled, tiled, P(), P()), out_specs=tiled, check_vma=False
    )
```

```python
import jax
import jax.numpy as jnp
from jax import lax
from jax.sharding import Mesh, PartitionSpec as P

RING = 16
HALVES = 2
SCALE = 2.0**21


def swap(block):
    return lax.ppermute(block, "half", [(0, 1), (1, 0)])


def parts_of(tile, half):
    rows = tile.shape[0] // HALVES
    halves = tile.reshape(HALVES, rows, tile.shape[1])
    return (
        lax.dynamic_index_in_dim(halves, half, 0, False),
        lax.dynamic_index_in_dim(halves, 1 - half, 0, False),
    )


def spread_panels(own, other, owners, half):
    slot = owners[:2].reshape(2, 1, 1)
    block = jnp.where(slot // RING == half, own[None], other[None])
    sent = jnp.where(slot % RING == lax.axis_index("z"), block, jnp.zeros_like(block))
    scaled = (sent.astype(jnp.float32) * SCALE).astype(jnp.float16)
    return lax.psum(scaled, "z")


def contract(left, right, dims):
    return lax.dot_general(left, right, (dims, ((), ())), preferred_element_type=jnp.float32)


def sum_over(part, axes):
    count = lax.axis_size(axes)
    cut = part.reshape((count, part.shape[0] // count) + part.shape[1:])
    share = jnp.sum(lax.all_to_all(cut, axes, 0, 0), axis=0)
    spread = jnp.broadcast_to(share[None], (count,) + share.shape)
    return lax.all_to_all(spread, axes, 0, 0).reshape(part.shape)


def exact(left, right):
    return lax.dot_general(
        left, right, (((1,), (1,)), ((), ())), precision=lax.Precision.HIGHEST,
        preferred_element_type=jnp.float32,
    )


def per_device(eigvecs, reflectors, factors, owners):
    columns = eigvecs.shape[1]
    half = lax.axis_index("half")
    own, away = parts_of(reflectors, half)
    other = swap(away)
    mine, guest = parts_of(eigvecs, half)
    theirs = swap(guest)
    whole = spread_panels(own, other, owners, half)
    panels = [whole[p].astype(jnp.bfloat16) for p in range(2)]

    blocks = []
    for p in range(2):
        here = contract(mine, panels[p], ((0,), (0,)))
        there = contract(theirs, panels[p], ((0,), (0,)))
        blocks += [jnp.where(half == 0, here, there), jnp.where(half == 0, there, here)]
    cross = contract(panels[1], panels[0], ((0,), (0,)))
    summed = sum_over(jnp.concatenate(blocks + [cross], axis=0), ("row", "half"))
    count = HALVES * columns
    first = summed[:count] * (1 / SCALE)
    second = summed[count : 2 * count] * (1 / SCALE)
    cross = summed[2 * count :] * (1 / SCALE**2)
    lead = exact(first, factors[0]).astype(jnp.bfloat16)
    rest = second - exact(lead.astype(jnp.float32), cross)
    tail = exact(rest, factors[1]).astype(jnp.bfloat16)
    coeffs = [part.reshape(HALVES, columns, part.shape[1]) for part in (lead, tail)]

    def updated(tile, which):
        total = tile.astype(jnp.float32)
        for p in range(2):
            part = lax.dynamic_index_in_dim(coeffs[p], which, 0, False)
            total = total - contract(panels[p], part, ((1,), (1,))) * (1 / SCALE)
        return total.astype(jnp.bfloat16)

    got = swap(updated(theirs, 1 - half))
    kept = updated(mine, half)
    first_rows = jnp.where(half == 0, kept, got)
    last_rows = jnp.where(half == 0, got, kept)
    return jnp.concatenate([first_rows, last_rows], axis=0)


def solution(mesh):
    fine = Mesh(mesh.devices.reshape(-1, HALVES, RING), ("row", "half", "z"))
    tiled = P("row", ("half", "z"))
    return jax.shard_map(
        per_device, mesh=fine, in_specs=(tiled, tiled, P(), P()), out_specs=tiled, check_vma=False
    )
```

```python
import jax
import jax.numpy as jnp
from jax import lax
from jax.sharding import Mesh, PartitionSpec as P

RING = 16
HALVES = 2
SCALE = 2.0**21


def swap(block, axis="half"):
    return lax.ppermute(block, axis, [(0, 1), (1, 0)])


def parts_of(tile, half):
    rows = tile.shape[0] // HALVES
    halves = tile.reshape(HALVES, rows, tile.shape[1])
    return (
        lax.dynamic_index_in_dim(halves, half, 0, False),
        lax.dynamic_index_in_dim(halves, 1 - half, 0, False),
    )


def spread_panels(own, other, owners, half):
    slot = owners[:2].reshape(2, 1, 1)
    block = jnp.where(slot // RING == half, own[None], other[None])
    sent = jnp.where(slot % RING == lax.axis_index("z"), block, jnp.zeros_like(block))
    scaled = (sent.astype(jnp.float32) * SCALE).astype(jnp.float16)
    return lax.psum(scaled, "z")


def contract(left, right, dims):
    return lax.dot_general(left, right, (dims, ((), ())), preferred_element_type=jnp.float32)


def sum_over_rows(part):
    axes = ("chip", "half")
    count = lax.axis_size(axes)
    cut = part.reshape((count, part.shape[0] // count) + part.shape[1:])
    share = jnp.sum(lax.all_to_all(cut, axes, 0, 0), axis=0)
    share = share + swap(share, "core")
    spread = jnp.broadcast_to(share[None], (count,) + share.shape)
    return lax.all_to_all(spread, axes, 0, 0).reshape(part.shape)


def exact(left, right):
    return lax.dot_general(
        left, right, (((1,), (1,)), ((), ())), precision=lax.Precision.HIGHEST,
        preferred_element_type=jnp.float32,
    )


def per_device(eigvecs, reflectors, factors, owners):
    columns = eigvecs.shape[1]
    half = lax.axis_index("half")
    own, away = parts_of(reflectors, half)
    other = swap(away)
    mine, guest = parts_of(eigvecs, half)
    theirs = swap(guest)
    whole = spread_panels(own, other, owners, half)
    panels = [whole[p].astype(jnp.bfloat16) for p in range(2)]

    blocks = []
    for p in range(2):
        here = contract(mine, panels[p], ((0,), (0,)))
        there = contract(theirs, panels[p], ((0,), (0,)))
        blocks += [jnp.where(half == 0, here, there), jnp.where(half == 0, there, here)]
    cross = contract(panels[1], panels[0], ((0,), (0,)))
    summed = sum_over_rows(jnp.concatenate(blocks + [cross], axis=0))
    count = HALVES * columns
    first = summed[:count] * (1 / SCALE)
    second = summed[count : 2 * count] * (1 / SCALE)
    cross = summed[2 * count :] * (1 / SCALE**2)
    lead = exact(first, factors[0]).astype(jnp.bfloat16)
    rest = second - exact(lead.astype(jnp.float32), cross)
    tail = exact(rest, factors[1]).astype(jnp.bfloat16)
    coeffs = [part.reshape(HALVES, columns, part.shape[1]) for part in (lead, tail)]

    def updated(tile, which):
        total = tile.astype(jnp.float32)
        for p in range(2):
            part = lax.dynamic_index_in_dim(coeffs[p], which, 0, False)
            total = total - contract(panels[p], part, ((1,), (1,))) * (1 / SCALE)
        return total.astype(jnp.bfloat16)

    got = swap(updated(theirs, 1 - half))
    kept = updated(mine, half)
    rows = kept.shape[0]
    result = lax.dynamic_update_slice_in_dim(jnp.zeros_like(eigvecs), kept, half * rows, 0)
    return lax.dynamic_update_slice_in_dim(result, got, (1 - half) * rows, 0)


def solution(mesh):
    fine = Mesh(mesh.devices.reshape(-1, 2, HALVES, RING), ("chip", "core", "half", "z"))
    tiled = P(("chip", "core"), ("half", "z"))
    return jax.shard_map(
        per_device, mesh=fine, in_specs=(tiled, tiled, P(), P()), out_specs=tiled, check_vma=False
    )
```

```python
import jax
import jax.numpy as jnp
from jax import lax
from jax.sharding import Mesh, PartitionSpec as P

RING = 16
HALVES = 2
SCALE = 2.0**21


def swap(block, axis="half"):
    return lax.ppermute(block, axis, [(0, 1), (1, 0)])


def parts_of(tile, half):
    rows = tile.shape[0] // HALVES
    halves = tile.reshape(HALVES, rows, tile.shape[1])
    return (
        lax.dynamic_index_in_dim(halves, half, 0, False),
        lax.dynamic_index_in_dim(halves, 1 - half, 0, False),
    )


def spread_panels(own, other, owners, half):
    slot = owners[:2].reshape(2, 1, 1)
    block = jnp.where(slot // RING == half, own[None], other[None])
    sent = jnp.where(slot % RING == lax.axis_index("z"), block, jnp.zeros_like(block))
    scaled = (sent.astype(jnp.float32) * SCALE).astype(jnp.float16)
    return lax.psum(scaled, "z")


def contract(left, right, dims):
    return lax.dot_general(left, right, (dims, ((), ())), preferred_element_type=jnp.float32)


def sum_over_rows(part):
    axes = ("chip", "half")
    count = lax.axis_size(axes)
    cut = part.reshape((count, part.shape[0] // count) + part.shape[1:])
    share = jnp.sum(lax.all_to_all(cut, axes, 0, 0), axis=0)
    share = share + swap(share, "core")
    spread = jnp.broadcast_to(share[None], (count,) + share.shape)
    return lax.all_to_all(spread, axes, 0, 0).reshape(part.shape)


def exact(left, right):
    return lax.dot_general(
        left, right, (((1,), (1,)), ((), ())), precision=lax.Precision.HIGHEST,
        preferred_element_type=jnp.float32,
    )


def per_device(eigvecs, reflectors, factors, owners):
    columns = eigvecs.shape[1]
    half = lax.axis_index("half")
    own, away = parts_of(reflectors, half)
    other = swap(away)
    mine, guest = parts_of(eigvecs, half)
    theirs = swap(guest)
    whole = spread_panels(own, other, owners, half)
    panels = [whole[p].astype(jnp.bfloat16) for p in range(2)]

    blocks = []
    for p in range(2):
        here = contract(mine, panels[p], ((0,), (0,)))
        there = contract(theirs, panels[p], ((0,), (0,)))
        blocks += [jnp.where(half == 0, here, there), jnp.where(half == 0, there, here)]
    cross = contract(panels[1], panels[0], ((0,), (0,)))
    summed = sum_over_rows(jnp.concatenate(blocks + [cross], axis=0))
    count = HALVES * columns
    first = summed[:count] * (1 / SCALE)
    second = summed[count : 2 * count] * (1 / SCALE)
    cross = summed[2 * count :] * (1 / SCALE**2)
    lead = exact(first, factors[0]).astype(jnp.bfloat16)
    rest = second - exact(lead.astype(jnp.float32), cross)
    tail = exact(rest, factors[1]).astype(jnp.bfloat16)
    coeffs = [part.reshape(HALVES, columns, part.shape[1]) for part in (lead, tail)]

    def updated(tile, which):
        total = tile.astype(jnp.float32)
        for p in range(2):
            part = lax.dynamic_index_in_dim(coeffs[p], which, 0, False)
            total = total - contract(panels[p], part, ((1,), (1,))) * (1 / SCALE)
        return total.astype(jnp.bfloat16)

    got = swap(updated(theirs, 1 - half))
    kept = updated(mine, half)
    rows = kept.shape[0]
    return lax.dynamic_update_slice_in_dim(
        jnp.concatenate([kept, kept], axis=0), got, (1 - half) * rows, 0
    )


def solution(mesh):
    fine = Mesh(mesh.devices.reshape(-1, 2, HALVES, RING), ("chip", "core", "half", "z"))
    tiled = P(("chip", "core"), ("half", "z"))
    return jax.shard_map(
        per_device, mesh=fine, in_specs=(tiled, tiled, P(), P()), out_specs=tiled, check_vma=False
    )
```

```python
import jax
import jax.numpy as jnp
from jax import lax
from jax.sharding import Mesh, PartitionSpec as P

RING = 16
HALVES = 2
SCALE = 2.0**21


def swap(block, axis="half"):
    return lax.ppermute(block, axis, [(0, 1), (1, 0)])


def parts_of(tile, half):
    rows = tile.shape[0] // HALVES
    halves = tile.reshape(HALVES, rows, tile.shape[1])
    return (
        lax.dynamic_index_in_dim(halves, half, 0, False),
        lax.dynamic_index_in_dim(halves, 1 - half, 0, False),
    )


def spread_panels(own, other, owners, half):
    slot = owners[:2].reshape(2, 1, 1)
    block = jnp.where(slot // RING == half, own[None], other[None])
    sent = jnp.where(slot % RING == lax.axis_index("z"), block, jnp.zeros_like(block))
    scaled = (sent.astype(jnp.float32) * SCALE).astype(jnp.float16)
    return lax.psum(scaled, "z")


def contract(left, right, dims):
    return lax.dot_general(left, right, (dims, ((), ())), preferred_element_type=jnp.float32)


def sum_over_rows(part):
    axes = ("chip", "half")
    count = lax.axis_size(axes)
    cut = part.reshape((count, part.shape[0] // count) + part.shape[1:])
    share = jnp.sum(lax.all_to_all(cut, axes, 0, 0), axis=0)
    share = share + swap(share, "core")
    spread = jnp.broadcast_to(share[None], (count,) + share.shape)
    return lax.all_to_all(spread, axes, 0, 0).reshape(part.shape)


def exact(left, right):
    return lax.dot_general(
        left, right, (((1,), (1,)), ((), ())), precision=lax.Precision.HIGHEST,
        preferred_element_type=jnp.float32,
    )


def per_device(eigvecs, reflectors, factors, owners):
    columns = eigvecs.shape[1]
    half = lax.axis_index("half")
    own, away = parts_of(reflectors, half)
    other = swap(away)
    mine, guest = parts_of(eigvecs, half)
    theirs = swap(guest)
    whole = spread_panels(own, other, owners, half)
    panels = [whole[p].astype(jnp.bfloat16) for p in range(2)]

    blocks = []
    for p in range(2):
        here = contract(mine, panels[p], ((0,), (0,)))
        there = contract(theirs, panels[p], ((0,), (0,)))
        blocks += [jnp.where(half == 0, here, there), jnp.where(half == 0, there, here)]
    cross = contract(panels[1], panels[0], ((0,), (0,)))
    summed = sum_over_rows(jnp.concatenate(blocks + [cross], axis=0))
    count = HALVES * columns
    first = summed[:count] * (1 / SCALE)
    second = summed[count : 2 * count] * (1 / SCALE)
    cross = summed[2 * count :] * (1 / SCALE**2)
    lead = exact(first, factors[0]).astype(jnp.bfloat16)
    rest = second - exact(lead.astype(jnp.float32), cross)
    tail = exact(rest, factors[1]).astype(jnp.bfloat16)
    coeffs = [part.reshape(HALVES, columns, part.shape[1]) for part in (lead, tail)]

    def updated(tile, which):
        total = tile.astype(jnp.float32)
        for p in range(2):
            part = lax.dynamic_index_in_dim(coeffs[p], which, 0, False)
            total = total - contract(panels[p], part, ((1,), (1,))) * (1 / SCALE)
        return total.astype(jnp.bfloat16)

    got = swap(updated(theirs, 1 - half))
    kept = updated(mine, half)
    both = jnp.stack([kept, kept])
    return lax.dynamic_update_index_in_dim(both, got, 1 - half, 0).reshape(eigvecs.shape)


def solution(mesh):
    fine = Mesh(mesh.devices.reshape(-1, 2, HALVES, RING), ("chip", "core", "half", "z"))
    tiled = P(("chip", "core"), ("half", "z"))
    return jax.shard_map(
        per_device, mesh=fine, in_specs=(tiled, tiled, P(), P()), out_specs=tiled, check_vma=False
    )
```

```python
import jax
import jax.numpy as jnp
from jax import lax
from jax.sharding import Mesh, PartitionSpec as P

RING = 16
HALVES = 2
SCALE = 2.0**21


def swap(block, axis="half"):
    return lax.ppermute(block, axis, [(0, 1), (1, 0)])


def part_of(tile, half):
    rows = tile.shape[0] // HALVES
    return lax.dynamic_index_in_dim(tile.reshape(HALVES, rows, tile.shape[1]), half, 0, False)


def scaled(block):
    return (block.astype(jnp.float32) * SCALE).astype(jnp.float16)


def spread_panels(own, other, owners, half):
    slot = owners[:2].reshape(2, 1, 1)
    block = jnp.where(slot // RING == half, own[None], other[None])
    sent = jnp.where(slot % RING == lax.axis_index("z"), block, jnp.zeros_like(block))
    return lax.psum(sent, "z")


def contract(left, right, dims):
    return lax.dot_general(left, right, (dims, ((), ())), preferred_element_type=jnp.float32)


def sum_over_rows(part):
    axes = ("chip", "half")
    count = lax.axis_size(axes)
    cut = part.reshape((count, part.shape[0] // count) + part.shape[1:])
    share = jnp.sum(lax.all_to_all(cut, axes, 0, 0), axis=0)
    share = share + swap(share, "core")
    spread = jnp.broadcast_to(share[None], (count,) + share.shape)
    return lax.all_to_all(spread, axes, 0, 0).reshape(part.shape)


def exact(left, right):
    return lax.dot_general(
        left, right, (((1,), (1,)), ((), ())), precision=lax.Precision.HIGHEST,
        preferred_element_type=jnp.float32,
    )


def per_device(eigvecs, reflectors, factors, owners):
    columns = eigvecs.shape[1]
    half = lax.axis_index("half")
    away = part_of(reflectors, 1 - half)
    other = swap(away)
    reflectors, _ = lax.optimization_barrier((reflectors, away))
    theirs = swap(part_of(eigvecs, 1 - half))
    own = scaled(part_of(reflectors, half))
    mine = part_of(eigvecs, half)
    own, mine, other = lax.optimization_barrier((own, mine, other))
    whole = spread_panels(own, scaled(other), owners, half)
    panels = [whole[p].astype(jnp.bfloat16) for p in range(2)]

    blocks = []
    for p in range(2):
        here = contract(mine, panels[p], ((0,), (0,)))
        there = contract(theirs, panels[p], ((0,), (0,)))
        blocks += [jnp.where(half == 0, here, there), jnp.where(half == 0, there, here)]
    cross = contract(panels[1], panels[0], ((0,), (0,)))
    summed = sum_over_rows(jnp.concatenate(blocks + [cross], axis=0))
    count = HALVES * columns
    first = summed[:count] * (1 / SCALE)
    second = summed[count : 2 * count] * (1 / SCALE)
    cross = summed[2 * count :] * (1 / SCALE**2)
    lead = exact(first, factors[0]).astype(jnp.bfloat16)
    rest = second - exact(lead.astype(jnp.float32), cross)
    tail = exact(rest, factors[1]).astype(jnp.bfloat16)
    coeffs = [part.reshape(HALVES, columns, part.shape[1]) for part in (lead, tail)]

    def updated(tile, which):
        total = tile.astype(jnp.float32)
        for p in range(2):
            part = lax.dynamic_index_in_dim(coeffs[p], which, 0, False)
            total = total - contract(panels[p], part, ((1,), (1,))) * (1 / SCALE)
        return total.astype(jnp.bfloat16)

    got = swap(updated(theirs, 1 - half))
    kept = updated(mine, half)
    both = jnp.stack([kept, kept])
    return lax.dynamic_update_index_in_dim(both, got, 1 - half, 0).reshape(eigvecs.shape)


def solution(mesh):
    fine = Mesh(mesh.devices.reshape(-1, 2, HALVES, RING), ("chip", "core", "half", "z"))
    tiled = P(("chip", "core"), ("half", "z"))
    return jax.shard_map(
        per_device, mesh=fine, in_specs=(tiled, tiled, P(), P()), out_specs=tiled, check_vma=False
    )
```

```python
import jax
import jax.numpy as jnp
from jax import lax
from jax.sharding import Mesh, PartitionSpec as P

RING = 16
HALVES = 2
SCALE = 2.0**21


def swap(block, axis="half"):
    return lax.ppermute(block, axis, [(0, 1), (1, 0)])


def part_of(tile, half):
    rows = tile.shape[0] // HALVES
    return lax.dynamic_index_in_dim(tile.reshape(HALVES, rows, tile.shape[1]), half, 0, False)


def spread_panels(own, other, owners, half):
    slot = owners[:2].reshape(2, 1, 1)
    block = jnp.where(slot // RING == half, own[None], other[None])
    sent = jnp.where(slot % RING == lax.axis_index("z"), block, jnp.zeros_like(block))
    scaled = (sent.astype(jnp.float32) * SCALE).astype(jnp.float16)
    return lax.psum(scaled, "z")


def contract(left, right, dims):
    return lax.dot_general(left, right, (dims, ((), ())), preferred_element_type=jnp.float32)


def sum_over_rows(part):
    axes = ("chip", "half")
    count = lax.axis_size(axes)
    cut = part.reshape((count, part.shape[0] // count) + part.shape[1:])
    share = jnp.sum(lax.all_to_all(cut, axes, 0, 0), axis=0)
    share = share + swap(share, "core")
    spread = jnp.broadcast_to(share[None], (count,) + share.shape)
    return lax.all_to_all(spread, axes, 0, 0).reshape(part.shape)


def exact(left, right):
    return lax.dot_general(
        left, right, (((1,), (1,)), ((), ())), precision=lax.Precision.HIGHEST,
        preferred_element_type=jnp.float32,
    )


def per_device(eigvecs, reflectors, factors, owners):
    columns = eigvecs.shape[1]
    half = lax.axis_index("half")
    away = part_of(reflectors, 1 - half)
    other = swap(away)
    reflectors, _ = lax.optimization_barrier((reflectors, away))
    theirs = swap(part_of(eigvecs, 1 - half))
    own = part_of(reflectors, half)
    mine = part_of(eigvecs, half)
    own, mine, other = lax.optimization_barrier((own, mine, other))
    whole = spread_panels(own, other, owners, half)
    panels = [whole[p].astype(jnp.bfloat16) for p in range(2)]

    blocks = []
    for p in range(2):
        here = contract(mine, panels[p], ((0,), (0,)))
        there = contract(theirs, panels[p], ((0,), (0,)))
        blocks += [jnp.where(half == 0, here, there), jnp.where(half == 0, there, here)]
    cross = contract(panels[1], panels[0], ((0,), (0,)))
    summed = sum_over_rows(jnp.concatenate(blocks + [cross], axis=0))
    count = HALVES * columns
    first = summed[:count] * (1 / SCALE)
    second = summed[count : 2 * count] * (1 / SCALE)
    cross = summed[2 * count :] * (1 / SCALE**2)
    lead = exact(first, factors[0]).astype(jnp.bfloat16)
    rest = second - exact(lead.astype(jnp.float32), cross)
    tail = exact(rest, factors[1]).astype(jnp.bfloat16)
    coeffs = [part.reshape(HALVES, columns, part.shape[1]) for part in (lead, tail)]

    def updated(tile, which):
        total = tile.astype(jnp.float32)
        for p in range(2):
            part = lax.dynamic_index_in_dim(coeffs[p], which, 0, False)
            total = total - contract(panels[p], part, ((1,), (1,))) * (1 / SCALE)
        return total.astype(jnp.bfloat16)

    got = swap(updated(theirs, 1 - half))
    kept = updated(mine, half)
    both = jnp.stack([kept, kept])
    return lax.dynamic_update_index_in_dim(both, got, 1 - half, 0).reshape(eigvecs.shape)


def solution(mesh):
    fine = Mesh(mesh.devices.reshape(-1, 2, HALVES, RING), ("chip", "core", "half", "z"))
    tiled = P(("chip", "core"), ("half", "z"))
    return jax.shard_map(
        per_device, mesh=fine, in_specs=(tiled, tiled, P(), P()), out_specs=tiled, check_vma=False
    )
```

```python
import jax
import jax.numpy as jnp
from jax import lax
from jax.sharding import Mesh, PartitionSpec as P

RING = 16
HALVES = 2
SCALE = 2.0**21


def swap(block, axis="half"):
    return lax.ppermute(block, axis, [(0, 1), (1, 0)])


def parts_of(tile, half):
    rows = tile.shape[0] // HALVES
    halves = tile.reshape(HALVES, rows, tile.shape[1])
    return (
        lax.dynamic_index_in_dim(halves, half, 0, False),
        lax.dynamic_index_in_dim(halves, 1 - half, 0, False),
    )


def spread_panels(own, other, owners, half):
    slot = owners[:2].reshape(2, 1, 1)
    block = jnp.where(slot // RING == half, own[None], other[None])
    sent = jnp.where(slot % RING == lax.axis_index("z"), block, jnp.zeros_like(block))
    scaled = (sent.astype(jnp.float32) * SCALE).astype(jnp.float16)
    return lax.psum(scaled, "z")


def contract(left, right, dims):
    return lax.dot_general(left, right, (dims, ((), ())), preferred_element_type=jnp.float32)


def sum_over_rows(part):
    axes = ("chip", "half")
    count = lax.axis_size(axes)
    cut = part.reshape((count, part.shape[0] // count) + part.shape[1:])
    share = jnp.sum(lax.all_to_all(cut, axes, 0, 0), axis=0)
    share = share + swap(share, "core")
    spread = jnp.broadcast_to(share[None], (count,) + share.shape)
    return lax.all_to_all(spread, axes, 0, 0).reshape(part.shape)


def exact(left, right):
    return lax.dot_general(
        left, right, (((1,), (1,)), ((), ())), precision=lax.Precision.HIGHEST,
        preferred_element_type=jnp.float32,
    )


def per_device(eigvecs, reflectors, factors, owners):
    columns = eigvecs.shape[1]
    half = lax.axis_index("half")
    own, away = parts_of(reflectors, half)
    other = swap(away)
    mine, guest = parts_of(eigvecs, half)
    theirs = swap(guest)
    mine, other = lax.optimization_barrier((mine, other))
    whole = spread_panels(own, other, owners, half)
    panels = [whole[p].astype(jnp.bfloat16) for p in range(2)]

    blocks = []
    for p in range(2):
        here = contract(mine, panels[p], ((0,), (0,)))
        there = contract(theirs, panels[p], ((0,), (0,)))
        blocks += [jnp.where(half == 0, here, there), jnp.where(half == 0, there, here)]
    cross = contract(panels[1], panels[0], ((0,), (0,)))
    summed = sum_over_rows(jnp.concatenate(blocks + [cross], axis=0))
    count = HALVES * columns
    first = summed[:count] * (1 / SCALE)
    second = summed[count : 2 * count] * (1 / SCALE)
    cross = summed[2 * count :] * (1 / SCALE**2)
    lead = exact(first, factors[0]).astype(jnp.bfloat16)
    rest = second - exact(lead.astype(jnp.float32), cross)
    tail = exact(rest, factors[1]).astype(jnp.bfloat16)
    coeffs = [part.reshape(HALVES, columns, part.shape[1]) for part in (lead, tail)]

    def updated(tile, which):
        total = tile.astype(jnp.float32)
        for p in range(2):
            part = lax.dynamic_index_in_dim(coeffs[p], which, 0, False)
            total = total - contract(panels[p], part, ((1,), (1,))) * (1 / SCALE)
        return total.astype(jnp.bfloat16)

    got = swap(updated(theirs, 1 - half))
    kept = updated(mine, half)
    both = jnp.stack([kept, kept])
    return lax.dynamic_update_index_in_dim(both, got, 1 - half, 0).reshape(eigvecs.shape)


def solution(mesh):
    fine = Mesh(mesh.devices.reshape(-1, 2, HALVES, RING), ("chip", "core", "half", "z"))
    tiled = P(("chip", "core"), ("half", "z"))
    return jax.shard_map(
        per_device, mesh=fine, in_specs=(tiled, tiled, P(), P()), out_specs=tiled, check_vma=False
    )
```

```python
import jax
import jax.numpy as jnp
from jax import lax
from jax.sharding import Mesh, PartitionSpec as P

RING = 16
HALVES = 2
SCALE = 2.0**21


def swap(block, axis="half"):
    return lax.ppermute(block, axis, [(0, 1), (1, 0)])


def part_of(tile, half):
    rows = tile.shape[0] // HALVES
    return lax.dynamic_index_in_dim(tile.reshape(HALVES, rows, tile.shape[1]), half, 0, False)


def scaled(block):
    return block.astype(jnp.float32) * SCALE


def spread_panels(own, other, owners, half):
    slot = owners[:2].reshape(2, 1, 1)
    block = jnp.where(slot // RING == half, own[None], other[None])
    sent = jnp.where(slot % RING == lax.axis_index("z"), block, jnp.zeros_like(block))
    return lax.psum(sent.astype(jnp.float16), "z")


def contract(left, right, dims):
    return lax.dot_general(left, right, (dims, ((), ())), preferred_element_type=jnp.float32)


def sum_over_rows(part):
    axes = ("chip", "half")
    count = lax.axis_size(axes)
    cut = part.reshape((count, part.shape[0] // count) + part.shape[1:])
    share = jnp.sum(lax.all_to_all(cut, axes, 0, 0), axis=0)
    share = share + swap(share, "core")
    spread = jnp.broadcast_to(share[None], (count,) + share.shape)
    return lax.all_to_all(spread, axes, 0, 0).reshape(part.shape)


def exact(left, right):
    return lax.dot_general(
        left, right, (((1,), (1,)), ((), ())), precision=lax.Precision.HIGHEST,
        preferred_element_type=jnp.float32,
    )


def per_device(eigvecs, reflectors, factors, owners):
    columns = eigvecs.shape[1]
    half = lax.axis_index("half")
    away = part_of(reflectors, 1 - half)
    other = swap(away)
    reflectors, _ = lax.optimization_barrier((reflectors, away))
    theirs = swap(part_of(eigvecs, 1 - half))
    own = scaled(part_of(reflectors, half))
    mine = part_of(eigvecs, half)
    own, mine, other = lax.optimization_barrier((own, mine, other))
    whole = spread_panels(own, scaled(other), owners, half)
    panels = [whole[p].astype(jnp.bfloat16) for p in range(2)]

    blocks = []
    for p in range(2):
        here = contract(mine, panels[p], ((0,), (0,)))
        there = contract(theirs, panels[p], ((0,), (0,)))
        blocks += [jnp.where(half == 0, here, there), jnp.where(half == 0, there, here)]
    cross = contract(panels[1], panels[0], ((0,), (0,)))
    summed = sum_over_rows(jnp.concatenate(blocks + [cross], axis=0))
    count = HALVES * columns
    first = summed[:count] * (1 / SCALE)
    second = summed[count : 2 * count] * (1 / SCALE)
    cross = summed[2 * count :] * (1 / SCALE**2)
    lead = exact(first, factors[0]).astype(jnp.bfloat16)
    rest = second - exact(lead.astype(jnp.float32), cross)
    tail = exact(rest, factors[1]).astype(jnp.bfloat16)
    coeffs = [part.reshape(HALVES, columns, part.shape[1]) for part in (lead, tail)]

    def updated(tile, which):
        total = tile.astype(jnp.float32)
        for p in range(2):
            part = lax.dynamic_index_in_dim(coeffs[p], which, 0, False)
            total = total - contract(panels[p], part, ((1,), (1,))) * (1 / SCALE)
        return total.astype(jnp.bfloat16)

    got = swap(updated(theirs, 1 - half))
    kept = updated(mine, half)
    both = jnp.stack([kept, kept])
    return lax.dynamic_update_index_in_dim(both, got, 1 - half, 0).reshape(eigvecs.shape)


def solution(mesh):
    fine = Mesh(mesh.devices.reshape(-1, 2, HALVES, RING), ("chip", "core", "half", "z"))
    tiled = P(("chip", "core"), ("half", "z"))
    return jax.shard_map(
        per_device, mesh=fine, in_specs=(tiled, tiled, P(), P()), out_specs=tiled, check_vma=False
    )
```

```python
import jax
import jax.numpy as jnp
from jax import lax
from jax.sharding import Mesh, PartitionSpec as P

RING = 16
HALVES = 2
SCALE = 2.0**21


TURN = ("core", "half", "z")


def device(core, half, z):
    return (core % 2 * HALVES + half % 2) * RING + z


TURNS = [
    [device(first + z, half, z) for z in range(RING)] for first in range(2) for half in range(HALVES)
]


def turn(block, across):
    pairs = [
        (device(core, half, z), device(core + z, half + across, z))
        for core in range(2)
        for half in range(HALVES)
        for z in range(RING)
    ]
    return lax.ppermute(block, TURN, pairs)


def parts_of(tile, half):
    rows = tile.shape[0] // HALVES
    halves = tile.reshape(HALVES, rows, tile.shape[1])
    return (
        lax.dynamic_index_in_dim(halves, half, 0, False),
        lax.dynamic_index_in_dim(halves, 1 - half, 0, False),
    )


def spread_panels(own, other, owners, half):
    slot = owners[:2].reshape(2, 1, 1)
    block = jnp.where(slot // RING == half, own[None], other[None])
    sent = jnp.where(slot % RING == lax.axis_index("z"), block, jnp.zeros_like(block))
    scaled = (sent.astype(jnp.float32) * SCALE).astype(jnp.float16)
    return lax.psum(scaled, TURN, axis_index_groups=TURNS)


def contract(left, right, dims):
    return lax.dot_general(left, right, (dims, ((), ())), preferred_element_type=jnp.float32)


def sum_over_rows(part):
    axes = ("chip", "half")
    count = lax.axis_size(axes)
    cut = part.reshape((count, part.shape[0] // count) + part.shape[1:])
    share = jnp.sum(lax.all_to_all(cut, axes, 0, 0), axis=0)
    share = share + lax.ppermute(share, "core", [(0, 1), (1, 0)])
    spread = jnp.broadcast_to(share[None], (count,) + share.shape)
    return lax.all_to_all(spread, axes, 0, 0).reshape(part.shape)


def exact(left, right):
    return lax.dot_general(
        left, right, (((1,), (1,)), ((), ())), precision=lax.Precision.HIGHEST,
        preferred_element_type=jnp.float32,
    )


def per_device(eigvecs, reflectors, factors, owners):
    columns = eigvecs.shape[1]
    half = lax.axis_index("half")
    own, away = parts_of(reflectors, half)
    other = turn(away, 1)
    mine, guest = parts_of(eigvecs, half)
    theirs = turn(guest, 1)
    own, mine = turn(own, 0), turn(mine, 0)
    whole = spread_panels(own, other, owners, half)
    panels = [whole[p].astype(jnp.bfloat16) for p in range(2)]

    blocks = []
    for p in range(2):
        here = contract(mine, panels[p], ((0,), (0,)))
        there = contract(theirs, panels[p], ((0,), (0,)))
        blocks += [jnp.where(half == 0, here, there), jnp.where(half == 0, there, here)]
    cross = contract(panels[1], panels[0], ((0,), (0,)))
    summed = sum_over_rows(jnp.concatenate(blocks + [cross], axis=0))
    count = HALVES * columns
    first = summed[:count] * (1 / SCALE)
    second = summed[count : 2 * count] * (1 / SCALE)
    cross = summed[2 * count :] * (1 / SCALE**2)
    lead = exact(first, factors[0]).astype(jnp.bfloat16)
    rest = second - exact(lead.astype(jnp.float32), cross)
    tail = exact(rest, factors[1]).astype(jnp.bfloat16)
    coeffs = [part.reshape(HALVES, columns, part.shape[1]) for part in (lead, tail)]

    def updated(tile, which):
        total = tile.astype(jnp.float32)
        for p in range(2):
            part = lax.dynamic_index_in_dim(coeffs[p], which, 0, False)
            total = total - contract(panels[p], part, ((1,), (1,))) * (1 / SCALE)
        return total.astype(jnp.bfloat16)

    got = turn(updated(theirs, 1 - half), 1)
    kept = turn(updated(mine, half), 0)
    both = jnp.stack([kept, kept])
    return lax.dynamic_update_index_in_dim(both, got, 1 - half, 0).reshape(eigvecs.shape)


def solution(mesh):
    fine = Mesh(mesh.devices.reshape(-1, 2, HALVES, RING), ("chip", "core", "half", "z"))
    tiled = P(("chip", "core"), ("half", "z"))
    return jax.shard_map(
        per_device, mesh=fine, in_specs=(tiled, tiled, P(), P()), out_specs=tiled, check_vma=False
    )
```

```python
import jax
import jax.numpy as jnp
from jax import lax
from jax.sharding import Mesh, PartitionSpec as P

RING = 16
HALVES = 2
SCALE = 2.0**21


TURN = ("core", "half", "z")


def device(core, half, z):
    return (core % 2 * HALVES + half % 2) * RING + z


TURNS = [
    [device(first + z, half, z) for z in range(RING)] for first in range(2) for half in range(HALVES)
]


def turn(block, across):
    pairs = [
        (device(core, half, z), device(core + z, half + across, z))
        for core in range(2)
        for half in range(HALVES)
        for z in range(RING)
    ]
    return lax.ppermute(block, TURN, pairs)


def parts_of(tile, half):
    rows = tile.shape[0] // HALVES
    halves = tile.reshape(HALVES, rows, tile.shape[1])
    return (
        lax.dynamic_index_in_dim(halves, half, 0, False),
        lax.dynamic_index_in_dim(halves, 1 - half, 0, False),
    )


def spread_panels(own, other, owners, half):
    slot = owners[:2].reshape(2, 1, 1)
    block = jnp.where(slot // RING == half, own[None], other[None])
    sent = jnp.where(slot % RING == lax.axis_index("z"), block, jnp.zeros_like(block))
    scaled = (sent.astype(jnp.float32) * SCALE).astype(jnp.float16)
    return lax.psum(scaled, TURN, axis_index_groups=TURNS)


def contract(left, right, dims):
    return lax.dot_general(left, right, (dims, ((), ())), preferred_element_type=jnp.float32)


def sum_over(part, axes):
    count = lax.axis_size(axes)
    cut = part.reshape((count, part.shape[0] // count) + part.shape[1:])
    share = jnp.sum(lax.all_to_all(cut, axes, 0, 0), axis=0)
    spread = jnp.broadcast_to(share[None], (count,) + share.shape)
    return lax.all_to_all(spread, axes, 0, 0).reshape(part.shape)


def exact(left, right):
    return lax.dot_general(
        left, right, (((1,), (1,)), ((), ())), precision=lax.Precision.HIGHEST,
        preferred_element_type=jnp.float32,
    )


def per_device(eigvecs, reflectors, factors, owners):
    columns = eigvecs.shape[1]
    half = lax.axis_index("half")
    own, away = parts_of(reflectors, half)
    other = turn(away, 1)
    mine, guest = parts_of(eigvecs, half)
    own, mine, guest = lax.optimization_barrier((own, mine, guest))
    theirs = turn(guest, 1)
    own, mine = turn(own, 0), turn(mine, 0)
    whole = spread_panels(own, other, owners, half)
    panels = [whole[p].astype(jnp.bfloat16) for p in range(2)]

    blocks = []
    for p in range(2):
        here = contract(mine, panels[p], ((0,), (0,)))
        there = contract(theirs, panels[p], ((0,), (0,)))
        blocks += [jnp.where(half == 0, here, there), jnp.where(half == 0, there, here)]
    cross = contract(panels[1], panels[0], ((0,), (0,)))
    summed = sum_over(jnp.concatenate(blocks + [cross], axis=0), ("chip", "core", "half"))
    count = HALVES * columns
    first = summed[:count] * (1 / SCALE)
    second = summed[count : 2 * count] * (1 / SCALE)
    cross = summed[2 * count :] * (1 / SCALE**2)
    lead = exact(first, factors[0]).astype(jnp.bfloat16)
    rest = second - exact(lead.astype(jnp.float32), cross)
    tail = exact(rest, factors[1]).astype(jnp.bfloat16)
    coeffs = [part.reshape(HALVES, columns, part.shape[1]) for part in (lead, tail)]

    def updated(tile, which):
        total = tile.astype(jnp.float32)
        for p in range(2):
            part = lax.dynamic_index_in_dim(coeffs[p], which, 0, False)
            total = total - contract(panels[p], part, ((1,), (1,))) * (1 / SCALE)
        return total.astype(jnp.bfloat16)

    sent, mine = lax.optimization_barrier((updated(theirs, 1 - half), mine))
    got = turn(sent, 1)
    kept = turn(updated(mine, half), 0)
    both = jnp.stack([kept, kept])
    return lax.dynamic_update_index_in_dim(both, got, 1 - half, 0).reshape(eigvecs.shape)


def solution(mesh):
    fine = Mesh(mesh.devices.reshape(-1, 2, HALVES, RING), ("chip", "core", "half", "z"))
    tiled = P(("chip", "core"), ("half", "z"))
    return jax.shard_map(
        per_device, mesh=fine, in_specs=(tiled, tiled, P(), P()), out_specs=tiled, check_vma=False
    )
```

```python
import jax
import jax.numpy as jnp
from jax import lax
from jax.sharding import Mesh, PartitionSpec as P

RING = 16
HALVES = 2
SCALE = 2.0**21


def swap(block, axis="half"):
    return lax.ppermute(block, axis, [(0, 1), (1, 0)])


def parts_of(tile, half):
    rows = tile.shape[0] // HALVES
    halves = tile.reshape(HALVES, rows, tile.shape[1])
    return (
        lax.dynamic_index_in_dim(halves, half, 0, False),
        lax.dynamic_index_in_dim(halves, 1 - half, 0, False),
    )


def spread_panels(own, other, owners, half):
    slot = owners[:2].reshape(2, 1, 1)
    block = jnp.where(slot // RING == half, own[None], other[None])
    sent = jnp.where(slot % RING == lax.axis_index("z"), block, jnp.zeros_like(block))
    scaled = (sent.astype(jnp.float32) * SCALE).astype(jnp.float16)
    return lax.psum(scaled, "z")


def contract(left, right, dims):
    return lax.dot_general(left, right, (dims, ((), ())), preferred_element_type=jnp.float32)


def sum_over_rows(part):
    axes = ("chip", "half")
    count = lax.axis_size(axes)
    cut = part.reshape((count, part.shape[0] // count) + part.shape[1:])
    share = jnp.sum(lax.all_to_all(cut, axes, 0, 0), axis=0)
    share = share + swap(share, "core")
    spread = jnp.broadcast_to(share[None], (count,) + share.shape)
    return lax.all_to_all(spread, axes, 0, 0).reshape(part.shape)


def exact(left, right):
    return lax.dot_general(
        left, right, (((1,), (1,)), ((), ())), precision=lax.Precision.HIGHEST,
        preferred_element_type=jnp.float32,
    )


def per_device(eigvecs, reflectors, factors, owners):
    columns = eigvecs.shape[1]
    half = lax.axis_index("half")
    own, away = parts_of(reflectors, half)
    other = swap(away)
    mine, guest = parts_of(eigvecs, half)
    theirs = swap(guest)
    early, other = lax.optimization_barrier((mine, other))
    whole = spread_panels(own, other, owners, half)
    panels = [whole[p].astype(jnp.bfloat16) for p in range(2)]

    blocks = []
    for p in range(2):
        here = contract(early, panels[p], ((0,), (0,)))
        there = contract(theirs, panels[p], ((0,), (0,)))
        blocks += [jnp.where(half == 0, here, there), jnp.where(half == 0, there, here)]
    cross = contract(panels[1], panels[0], ((0,), (0,)))
    summed = sum_over_rows(jnp.concatenate(blocks + [cross], axis=0))
    count = HALVES * columns
    first = summed[:count] * (1 / SCALE)
    second = summed[count : 2 * count] * (1 / SCALE)
    cross = summed[2 * count :] * (1 / SCALE**2)
    lead = exact(first, factors[0]).astype(jnp.bfloat16)
    rest = second - exact(lead.astype(jnp.float32), cross)
    tail = exact(rest, factors[1]).astype(jnp.bfloat16)
    coeffs = [part.reshape(HALVES, columns, part.shape[1]) for part in (lead, tail)]

    def updated(tile, which):
        total = tile.astype(jnp.float32)
        for p in range(2):
            part = lax.dynamic_index_in_dim(coeffs[p], which, 0, False)
            total = total - contract(panels[p], part, ((1,), (1,))) * (1 / SCALE)
        return total.astype(jnp.bfloat16)

    got = swap(updated(theirs, 1 - half))
    kept = updated(mine, half)
    both = jnp.stack([kept, kept])
    return lax.dynamic_update_index_in_dim(both, got, 1 - half, 0).reshape(eigvecs.shape)


def solution(mesh):
    fine = Mesh(mesh.devices.reshape(-1, 2, HALVES, RING), ("chip", "core", "half", "z"))
    tiled = P(("chip", "core"), ("half", "z"))
    return jax.shard_map(
        per_device, mesh=fine, in_specs=(tiled, tiled, P(), P()), out_specs=tiled, check_vma=False
    )
```

```python
import jax
import jax.numpy as jnp
from jax import lax
from jax.sharding import Mesh, PartitionSpec as P

RING = 16
HALVES = 2
SCALE = 2.0**21


def swap(block, axis="half"):
    return lax.ppermute(block, axis, [(0, 1), (1, 0)])


def part_of(tile, half):
    rows = tile.shape[0] // HALVES
    return lax.dynamic_index_in_dim(tile.reshape(HALVES, rows, tile.shape[1]), half, 0, False)


def scaled(block):
    return (block.astype(jnp.float32) * SCALE).astype(jnp.float16)


def spread_panels(own, other, owners, half):
    slot = owners[:2].reshape(2, 1, 1)
    block = jnp.where(slot // RING == half, own[None], other[None])
    sent = jnp.where(slot % RING == lax.axis_index("z"), block, jnp.zeros_like(block))
    return lax.psum(sent, "z")


def contract(left, right, dims):
    return lax.dot_general(left, right, (dims, ((), ())), preferred_element_type=jnp.float32)


def sum_over_rows(part):
    axes = ("chip", "half")
    count = lax.axis_size(axes)
    cut = part.reshape((count, part.shape[0] // count) + part.shape[1:])
    share = jnp.sum(lax.all_to_all(cut, axes, 0, 0), axis=0)
    share = share + swap(share, "core")
    spread = jnp.broadcast_to(share[None], (count,) + share.shape)
    return lax.all_to_all(spread, axes, 0, 0).reshape(part.shape)


def exact(left, right):
    return lax.dot_general(
        left, right, (((1,), (1,)), ((), ())), precision=lax.Precision.HIGHEST,
        preferred_element_type=jnp.float32,
    )


def per_device(eigvecs, reflectors, factors, owners):
    columns = eigvecs.shape[1]
    half = lax.axis_index("half")
    away = part_of(reflectors, 1 - half)
    other = swap(away)
    reflectors, _ = lax.optimization_barrier((reflectors, away))
    theirs = swap(part_of(eigvecs, 1 - half))
    own = scaled(part_of(reflectors, half))
    mine = part_of(eigvecs, half)
    own, early, other = lax.optimization_barrier((own, mine, other))
    whole = spread_panels(own, scaled(other), owners, half)
    panels = [whole[p].astype(jnp.bfloat16) for p in range(2)]

    blocks = []
    for p in range(2):
        here = contract(early, panels[p], ((0,), (0,)))
        there = contract(theirs, panels[p], ((0,), (0,)))
        blocks += [jnp.where(half == 0, here, there), jnp.where(half == 0, there, here)]
    cross = contract(panels[1], panels[0], ((0,), (0,)))
    summed = sum_over_rows(jnp.concatenate(blocks + [cross], axis=0))
    count = HALVES * columns
    first = summed[:count] * (1 / SCALE)
    second = summed[count : 2 * count] * (1 / SCALE)
    cross = summed[2 * count :] * (1 / SCALE**2)
    lead = exact(first, factors[0]).astype(jnp.bfloat16)
    rest = second - exact(lead.astype(jnp.float32), cross)
    tail = exact(rest, factors[1]).astype(jnp.bfloat16)
    coeffs = [part.reshape(HALVES, columns, part.shape[1]) for part in (lead, tail)]

    def updated(tile, which):
        total = tile.astype(jnp.float32)
        for p in range(2):
            part = lax.dynamic_index_in_dim(coeffs[p], which, 0, False)
            total = total - contract(panels[p], part, ((1,), (1,))) * (1 / SCALE)
        return total.astype(jnp.bfloat16)

    got = swap(updated(theirs, 1 - half))
    kept = updated(mine, half)
    both = jnp.stack([kept, kept])
    return lax.dynamic_update_index_in_dim(both, got, 1 - half, 0).reshape(eigvecs.shape)


def solution(mesh):
    fine = Mesh(mesh.devices.reshape(-1, 2, HALVES, RING), ("chip", "core", "half", "z"))
    tiled = P(("chip", "core"), ("half", "z"))
    return jax.shard_map(
        per_device, mesh=fine, in_specs=(tiled, tiled, P(), P()), out_specs=tiled, check_vma=False
    )
```

```python
import jax
import jax.numpy as jnp
from jax import lax
from jax.sharding import Mesh, PartitionSpec as P

RING = 16
HALVES = 2
SCALE = 2.0**21


TURN = ("core", "half", "z")


def device(core, half, z):
    return (core % 2 * HALVES + half % 2) * RING + z


TURNS = [
    [device(first + z, half, z) for z in range(RING)] for first in range(2) for half in range(HALVES)
]


def turn(block, across):
    pairs = [
        (device(core, half, z), device(core + z, half + across, z))
        for core in range(2)
        for half in range(HALVES)
        for z in range(RING)
    ]
    return lax.ppermute(block, TURN, pairs)


def parts_of(tile, half):
    rows = tile.shape[0] // HALVES
    halves = tile.reshape(HALVES, rows, tile.shape[1])
    return (
        lax.dynamic_index_in_dim(halves, half, 0, False),
        lax.dynamic_index_in_dim(halves, 1 - half, 0, False),
    )


def spread_panels(own, other, owners, half):
    slot = owners[:2].reshape(2, 1, 1)
    block = jnp.where(slot // RING != half, other[None], own[None])
    sent = jnp.where(slot % RING == lax.axis_index("z"), block, jnp.zeros_like(block))
    scaled = (sent.astype(jnp.float32) * SCALE).astype(jnp.float16)
    return lax.psum(scaled, TURN, axis_index_groups=TURNS)


def contract(left, right, dims):
    return lax.dot_general(left, right, (dims, ((), ())), preferred_element_type=jnp.float32)


def sum_over(part, axes):
    count = lax.axis_size(axes)
    cut = part.reshape((count, part.shape[0] // count) + part.shape[1:])
    share = jnp.sum(lax.all_to_all(cut, axes, 0, 0), axis=0)
    spread = jnp.broadcast_to(share[None], (count,) + share.shape)
    return lax.all_to_all(spread, axes, 0, 0).reshape(part.shape)


def exact(left, right):
    return lax.dot_general(
        left, right, (((1,), (1,)), ((), ())), precision=lax.Precision.HIGHEST,
        preferred_element_type=jnp.float32,
    )


def per_device(eigvecs, reflectors, factors, owners):
    columns = eigvecs.shape[1]
    half = lax.axis_index("half")
    own, away = parts_of(reflectors, half)
    own = turn(own, 0)
    other = turn(away, 1)
    mine, guest = parts_of(eigvecs, half)
    theirs, mine = turn(guest, 1), turn(mine, 0)
    whole = spread_panels(own, other, owners, half)
    panels = [whole[p].astype(jnp.bfloat16) for p in range(2)]

    blocks = []
    for p in range(2):
        here = contract(mine, panels[p], ((0,), (0,)))
        there = contract(theirs, panels[p], ((0,), (0,)))
        blocks += [jnp.where(half == 0, here, there), jnp.where(half == 0, there, here)]
    cross = contract(panels[1], panels[0], ((0,), (0,)))
    summed = sum_over(jnp.concatenate(blocks + [cross], axis=0), ("chip", "core", "half"))
    count = HALVES * columns
    first = summed[:count] * (1 / SCALE)
    second = summed[count : 2 * count] * (1 / SCALE)
    cross = summed[2 * count :] * (1 / SCALE**2)
    lead = exact(first, factors[0]).astype(jnp.bfloat16)
    rest = second - exact(lead.astype(jnp.float32), cross)
    tail = exact(rest, factors[1]).astype(jnp.bfloat16)
    coeffs = [part.reshape(HALVES, columns, part.shape[1]) for part in (lead, tail)]

    def updated(tile, which):
        total = tile.astype(jnp.float32)
        for p in range(2):
            part = lax.dynamic_index_in_dim(coeffs[p], which, 0, False)
            total = total - contract(panels[p], part, ((1,), (1,))) * (1 / SCALE)
        return total.astype(jnp.bfloat16)

    kept = turn(updated(mine, half), 0)
    got = turn(updated(theirs, 1 - half), 1)
    both = jnp.stack([kept, kept])
    return lax.dynamic_update_index_in_dim(both, got, 1 - half, 0).reshape(eigvecs.shape)


def solution(mesh):
    fine = Mesh(mesh.devices.reshape(-1, 2, HALVES, RING), ("chip", "core", "half", "z"))
    tiled = P(("chip", "core"), ("half", "z"))
    return jax.shard_map(
        per_device, mesh=fine, in_specs=(tiled, tiled, P(), P()), out_specs=tiled, check_vma=False
    )
```

```python
import jax
import jax.numpy as jnp
from jax import lax
from jax.sharding import Mesh, PartitionSpec as P

RING = 16
HALVES = 2
SCALE = 2.0**21


def swap(block, axis="half"):
    return lax.ppermute(block, axis, [(0, 1), (1, 0)])


def parts_of(tile, half):
    rows = tile.shape[0] // HALVES
    halves = tile.reshape(HALVES, rows, tile.shape[1])
    return (
        lax.dynamic_index_in_dim(halves, half, 0, False),
        lax.dynamic_index_in_dim(halves, 1 - half, 0, False),
    )


def spread_panels(own, other, owners, half):
    slot = owners[:2].reshape(2, 1, 1)
    block = jnp.where(slot // RING == half, own[None], other[None])
    sent = jnp.where(slot % RING == lax.axis_index("z"), block, jnp.zeros_like(block))
    scaled = (sent.astype(jnp.float32) * SCALE).astype(jnp.float16)
    return lax.psum(scaled, "z")


def contract(left, right, dims):
    return lax.dot_general(left, right, (dims, ((), ())), preferred_element_type=jnp.float32)


def sum_over_rows(part):
    axes = ("chip", "half")
    count = lax.axis_size(axes)
    cut = part.reshape((count, part.shape[0] // count) + part.shape[1:])
    share = jnp.sum(lax.all_to_all(cut, axes, 0, 0), axis=0)
    share = share + swap(share, "core")
    spread = jnp.broadcast_to(share[None], (count,) + share.shape)
    return lax.all_to_all(spread, axes, 0, 0).reshape(part.shape)


def exact(left, right):
    return lax.dot_general(
        left, right, (((1,), (1,)), ((), ())), precision=lax.Precision.HIGHEST,
        preferred_element_type=jnp.float32,
    )


def per_device(eigvecs, reflectors, factors, owners):
    columns = eigvecs.shape[1]
    half = lax.axis_index("half")
    own, away = parts_of(reflectors, half)
    other = swap(away)
    mine, guest = parts_of(eigvecs, half)
    theirs = swap(guest)
    early, other = lax.optimization_barrier((mine, other))
    whole = spread_panels(own, other, owners, half)
    panels = [whole[p].astype(jnp.bfloat16) for p in range(2)]

    blocks = []
    for p in range(2):
        here = contract(early, panels[p], ((0,), (0,)))
        there = contract(theirs, panels[p], ((0,), (0,)))
        blocks += [jnp.where(half == 0, here, there), jnp.where(half == 0, there, here)]
    cross = contract(panels[1], panels[0], ((0,), (0,)))
    summed = sum_over_rows(jnp.concatenate(blocks + [cross], axis=0))
    count = HALVES * columns
    first = summed[:count] * (1 / SCALE)
    second = summed[count : 2 * count] * (1 / SCALE)
    cross = summed[2 * count :] * (1 / SCALE**2)
    lead = exact(first, factors[0]).astype(jnp.bfloat16)
    rest = second - exact(lead.astype(jnp.float32), cross)
    tail = exact(rest, factors[1]).astype(jnp.bfloat16)
    coeffs = [part.reshape(HALVES, columns, part.shape[1]) for part in (lead, tail)]

    def updated(tile, which):
        part = jnp.stack([lax.dynamic_index_in_dim(c, which, 0, False) for c in coeffs])
        update = contract(whole.astype(jnp.bfloat16), part, ((0, 2), (0, 2)))
        return (tile.astype(jnp.float32) - update * (1 / SCALE)).astype(jnp.bfloat16)

    got = swap(updated(theirs, 1 - half))
    kept = updated(mine, half)
    both = jnp.stack([kept, kept])
    return lax.dynamic_update_index_in_dim(both, got, 1 - half, 0).reshape(eigvecs.shape)


def solution(mesh):
    fine = Mesh(mesh.devices.reshape(-1, 2, HALVES, RING), ("chip", "core", "half", "z"))
    tiled = P(("chip", "core"), ("half", "z"))
    return jax.shard_map(
        per_device, mesh=fine, in_specs=(tiled, tiled, P(), P()), out_specs=tiled, check_vma=False
    )
```

```python
import jax
import jax.numpy as jnp
from jax import lax
from jax.sharding import Mesh, PartitionSpec as P

RING = 16
HALVES = 2
SCALE = 2.0**21


def swap(block, axis="half"):
    return lax.ppermute(block, axis, [(0, 1), (1, 0)])


def parts_of(tile, half):
    rows = tile.shape[0] // HALVES
    halves = tile.reshape(HALVES, rows, tile.shape[1])
    return (
        lax.dynamic_index_in_dim(halves, half, 0, False),
        lax.dynamic_index_in_dim(halves, 1 - half, 0, False),
    )


def spread_panels(own, other, owners, half):
    slot = owners[:2].reshape(2, 1, 1)
    block = jnp.where(slot // RING == half, own[None], other[None])
    sent = jnp.where(slot % RING == lax.axis_index("z"), block, jnp.zeros_like(block))
    scaled = (sent.astype(jnp.float32) * SCALE).astype(jnp.float16)
    return lax.psum(scaled, "z")


def contract(left, right, dims):
    return lax.dot_general(left, right, (dims, ((), ())), preferred_element_type=jnp.float32)


def sum_over_rows(part):
    axes = ("chip", "half")
    count = lax.axis_size(axes)
    cut = part.reshape((count, part.shape[0] // count) + part.shape[1:])
    share = jnp.sum(lax.all_to_all(cut, axes, 0, 0), axis=0)
    share = share + swap(share, "core")
    spread = jnp.broadcast_to(share[None], (count,) + share.shape)
    return lax.all_to_all(spread, axes, 0, 0).reshape(part.shape)


def exact(left, right):
    return lax.dot_general(
        left, right, (((1,), (1,)), ((), ())), precision=lax.Precision.HIGHEST,
        preferred_element_type=jnp.float32,
    )


def per_device(eigvecs, reflectors, factors, owners):
    columns = eigvecs.shape[1]
    half = lax.axis_index("half")
    own, away = parts_of(reflectors, half)
    other = swap(away)
    mine, guest = parts_of(eigvecs, half)
    theirs = swap(guest)
    early, other = lax.optimization_barrier((mine, other))
    whole = spread_panels(own, other, owners, half)
    panels = [whole[p].astype(jnp.bfloat16) for p in range(2)]

    here = contract(whole.astype(jnp.bfloat16), early, ((1,), (0,)))
    there = contract(whole.astype(jnp.bfloat16), theirs, ((1,), (0,)))
    blocks = []
    for p in range(2):
        blocks += [jnp.where(half == 0, here[p].T, there[p].T), jnp.where(half == 0, there[p].T, here[p].T)]
    cross = contract(panels[1], panels[0], ((0,), (0,)))
    summed = sum_over_rows(jnp.concatenate(blocks + [cross], axis=0))
    count = HALVES * columns
    first = summed[:count] * (1 / SCALE)
    second = summed[count : 2 * count] * (1 / SCALE)
    cross = summed[2 * count :] * (1 / SCALE**2)
    lead = exact(first, factors[0]).astype(jnp.bfloat16)
    rest = second - exact(lead.astype(jnp.float32), cross)
    tail = exact(rest, factors[1]).astype(jnp.bfloat16)
    coeffs = [part.reshape(HALVES, columns, part.shape[1]) for part in (lead, tail)]

    def updated(tile, which):
        part = jnp.stack([lax.dynamic_index_in_dim(c, which, 0, False) for c in coeffs])
        update = contract(whole.astype(jnp.bfloat16), part, ((0, 2), (0, 2)))
        return (tile.astype(jnp.float32) - update * (1 / SCALE)).astype(jnp.bfloat16)

    got = swap(updated(theirs, 1 - half))
    kept = updated(mine, half)
    both = jnp.stack([kept, kept])
    return lax.dynamic_update_index_in_dim(both, got, 1 - half, 0).reshape(eigvecs.shape)


def solution(mesh):
    fine = Mesh(mesh.devices.reshape(-1, 2, HALVES, RING), ("chip", "core", "half", "z"))
    tiled = P(("chip", "core"), ("half", "z"))
    return jax.shard_map(
        per_device, mesh=fine, in_specs=(tiled, tiled, P(), P()), out_specs=tiled, check_vma=False
    )
```

```python
import jax
import jax.numpy as jnp
from jax import lax
from jax.sharding import Mesh, PartitionSpec as P

RING = 16
HALVES = 2
SCALE = 2.0**21


def swap(block, axis="half"):
    return lax.ppermute(block, axis, [(0, 1), (1, 0)])


def parts_of(tile, half):
    rows = tile.shape[0] // HALVES
    halves = tile.reshape(HALVES, rows, tile.shape[1])
    return (
        lax.dynamic_index_in_dim(halves, half, 0, False),
        lax.dynamic_index_in_dim(halves, 1 - half, 0, False),
    )


def spread_panels(own, other, owners, half):
    slot = owners[:2].reshape(2, 1, 1)
    block = jnp.where(slot // RING != half, other[None], own[None])
    sent = jnp.where(slot % RING == lax.axis_index("z"), block, jnp.zeros_like(block))
    scaled = (sent.astype(jnp.float32) * SCALE).astype(jnp.float16)
    return lax.psum(scaled, "z")


def contract(left, right, dims):
    return lax.dot_general(left, right, (dims, ((), ())), preferred_element_type=jnp.float32)


def sum_over_rows(part):
    axes = ("chip", "half")
    count = lax.axis_size(axes)
    cut = part.reshape((count, part.shape[0] // count) + part.shape[1:])
    share = jnp.sum(lax.all_to_all(cut, axes, 0, 0), axis=0)
    share = share + swap(share, "core")
    spread = jnp.broadcast_to(share[None], (count,) + share.shape)
    return lax.all_to_all(spread, axes, 0, 0).reshape(part.shape)


def exact(left, right):
    return lax.dot_general(
        left, right, (((1,), (1,)), ((), ())), precision=lax.Precision.HIGHEST,
        preferred_element_type=jnp.float32,
    )


def per_device(eigvecs, reflectors, factors, owners):
    columns = eigvecs.shape[1]
    half = lax.axis_index("half")
    own, away = parts_of(reflectors, half)
    other = swap(away)
    mine, guest = parts_of(eigvecs, half)
    theirs = swap(guest)
    early, other = lax.optimization_barrier((mine, other))
    whole = spread_panels(own, other, owners, half)
    panels = [whole[p].astype(jnp.bfloat16) for p in range(2)]

    blocks = []
    for p in range(2):
        here = contract(early, panels[p], ((0,), (0,)))
        there = contract(theirs, panels[p], ((0,), (0,)))
        blocks += [jnp.where(half == 0, here, there), jnp.where(half == 0, there, here)]
    cross = contract(panels[1], panels[0], ((0,), (0,)))
    summed = sum_over_rows(jnp.concatenate(blocks + [cross], axis=0))
    count = HALVES * columns
    first = summed[:count] * (1 / SCALE)
    second = summed[count : 2 * count] * (1 / SCALE)
    cross = summed[2 * count :] * (1 / SCALE**2)
    lead = exact(first, factors[0]).astype(jnp.bfloat16)
    rest = second - exact(lead.astype(jnp.float32), cross)
    tail = exact(rest, factors[1]).astype(jnp.bfloat16)
    coeffs = [part.reshape(HALVES, columns, part.shape[1]) for part in (lead, tail)]

    def updated(tile, which):
        part = jnp.stack([lax.dynamic_index_in_dim(c, which, 0, False) for c in coeffs])
        update = contract(whole.astype(jnp.bfloat16), part, ((0, 2), (0, 2)))
        return (tile.astype(jnp.float32) - update * (1 / SCALE)).astype(jnp.bfloat16)

    got = swap(updated(theirs, 1 - half))
    kept = updated(mine, half)
    both = jnp.stack([kept, kept])
    return lax.dynamic_update_index_in_dim(both, got, 1 - half, 0).reshape(eigvecs.shape)


def solution(mesh):
    fine = Mesh(mesh.devices.reshape(-1, 2, HALVES, RING), ("chip", "core", "half", "z"))
    tiled = P(("chip", "core"), ("half", "z"))
    return jax.shard_map(
        per_device, mesh=fine, in_specs=(tiled, tiled, P(), P()), out_specs=tiled, check_vma=False
    )
```
